32 devices in a mesh: parts: 2 (over y), seq: 4 (over z), head: 2 (over x), sub: 2 (over core).
Axes of the slice: x: 2, y: 2, z: 4, core: 2. Of those that a mesh axis runs over, the one named last changes fastest.
Arguments:
- queries: bfloat16 [2560, 4096], P(('parts', 'seq', 'sub'), 'head'), parts along dimension 0, may hold values from -256 to 256
- keys: bfloat16 [2560, 4096], P(('parts', 'seq', 'sub'), 'head'), parts along dimension 0, may hold values from -8 to 8
- values: bfloat16 [2560, 4096], P(('parts', 'seq', 'sub'), 'head'), parts along dimension 0, may hold values from -6 to 6
- bank: float32 [512, 128], replicated, may hold values from -6 to 6
- seeds: int32 [8, 32, 8], P('parts', 'head'), parts along dimension 0, may hold values from 0 to 511
- reach: int32 [64], P(('parts', 'head')), parts along dimension 0, may hold values from 1 to 8, as said below
Outputs:
- attended: bfloat16 [2560, 4096], P(('parts', 'seq', 'sub'), 'head'), parts along dimension 0
The draws below stay inside these ranges and needn't reach their ends.
There are 2 independent parts, one for each index of `parts`. The reference program is written for one: setup_inputs(seed, part) draws one part's arguments, and reference() takes and returns one part's arrays. A program takes and returns all parts, laid end to end along the dimension named above; an argument that names none is the same for every part. Nothing has to cross between parts.
Inputs may be any that keep to these rules, and one draw needn't show every extreme that they name: `reach`: some head has 8 and some head has 1.
All inputs are finite; a program needn't handle non-finite values.
Results may differ from the reference program's by a relative error of at most 0.0064.
Values may be sent and summed in bfloat16 or wider, within the bound.
A program may use at most 64 MiB of HBM per device.

```python
import jax
import jax.numpy as jnp
from jax import lax

HEADS = 32
HD = 128
REFL = 8
BANK = 512
WINDOW = 8
SHARD = 320
SHARDS = 4
SEQLEN = 1280


def drawn_pair(key):
    base = jax.random.fold_in(key, 7)
    key_query, key_key = jax.random.split(base, 2)
    key_field = jnp.clip(jax.random.normal(key_key, (SEQLEN, HEADS * HD), jnp.float32), -6.0, 6.0)
    query_field = 2.5 * jnp.clip(jax.random.normal(key_query, (SEQLEN, HEADS * HD), jnp.float32), -6.0, 6.0)
    return (query_field, key_field)


def draw_queries(key, part):
    return drawn_pair(key)[0].astype(jnp.bfloat16)


def draw_keys(key, part):
    return drawn_pair(key)[1].astype(jnp.bfloat16)


def draw_reach(key, part):
    base = jax.random.randint(jax.random.fold_in(key, 11), (HEADS,), 1, WINDOW + 1, dtype=jnp.int32)
    order = jax.random.permutation(jax.random.fold_in(key, 13), HEADS)
    return base.at[order[0]].set(WINDOW).at[order[1]].set(1)


def plant(values, stream_key, low, high):
    spot = [jax.random.randint(jax.random.fold_in(stream_key, axis), (), 0, length) for axis, length in enumerate(values.shape)]
    main_axis = values.shape.index(max(values.shape))
    neighbour = spot[:main_axis] + [(spot[main_axis] + 1) % values.shape[main_axis]] + spot[main_axis + 1:]
    return values.at[tuple(spot)].set(low).at[tuple(neighbour)].set(high)


def level_of(stream_key, dims, shards, low, top_value):
    def one(axis_at, blocks):
        steps = jax.random.uniform(jax.random.fold_in(jax.random.fold_in(stream_key, 6), axis_at), (blocks,), jnp.float32, low / len(shards), top_value / len(shards))
        return jnp.repeat(jnp.exp(steps), dims[axis_at] // blocks).reshape((-1,) + (1,) * (len(dims) - axis_at - 1))

    gain = one(*shards[0])
    for cut in shards[1:]:
        gain = gain * one(*cut)
    return gain


def normal_values(rng, dims, scale, bound, pieces=(), kind=jnp.bfloat16):
    level = level_of(rng, dims, pieces, -0.22, 0.18) if pieces else 1.0
    values = jax.random.normal(rng, dims, jnp.float32) * scale * level
    return jnp.minimum(jnp.maximum(values, -bound), bound).astype(kind)


def setup_inputs(seed: int = 0, part: int = 0) -> dict:
    key_of = jax.random.split(jax.random.key(seed), 7)
    part_keys = jax.random.split(jax.random.fold_in(key_of[6], part), 7)
    return {
        "queries": draw_queries(jax.random.fold_in(jax.random.fold_in(key_of[6], part), 71), part),
        "keys": draw_keys(jax.random.fold_in(jax.random.fold_in(key_of[6], part), 71), part),
        "values": normal_values(part_keys[2], (SEQLEN, HEADS * HD), 1.0, 6.0, ((0, 8), (1, 2))),
        "bank": normal_values(key_of[3], (BANK, HD), 1.0, 6.0, (), jnp.float32),
        "seeds": plant(jax.random.randint(part_keys[4], (SHARDS, HEADS, REFL), 0, BANK), jax.random.fold_in(part_keys[4], 1), 0, BANK - 1).astype(jnp.int32),
        "reach": draw_reach(jax.random.fold_in(jax.random.fold_in(key_of[6], part), 71), part),
    }


def reflect(vectors):
    width = vectors.shape[1]

    def apply_one(matrix, vector):
        image = jnp.dot(matrix, vector, precision=lax.Precision.HIGHEST)
        factor = 2.0 / (jnp.sum(vector * vector) + 1e-6)
        return matrix - factor * jnp.outer(image, vector), None

    start = jnp.eye(width, dtype=jnp.float32)
    result, ignored = lax.scan(apply_one, start, vectors)
    return result


def attend_block(query_heads, key_heads, value_heads, allowed, scale):
    scores = jnp.einsum("thx,khx->htk", query_heads.astype(jnp.float32), key_heads.astype(jnp.float32)) * scale
    if allowed is not None:
        scores = jnp.where(allowed[None], scores, -1e30)
    peak = jnp.max(scores, axis=-1)
    exp_terms = jnp.exp(scores - peak[..., None])
    total = jnp.sum(exp_terms, axis=-1)
    weights = exp_terms.astype(jnp.bfloat16)
    summed = jnp.einsum("htk,khx->thx", weights.astype(jnp.float32), value_heads.astype(jnp.float32))
    output = (summed / jnp.transpose(total)[..., None]).astype(jnp.bfloat16)
    return output, jnp.transpose(peak), jnp.transpose(total)


def weigh(output, peak, total, live):
    peak = jnp.where(live[None, :], peak, -1e30)
    total = total * live.astype(jnp.float32)[None, :]
    return total[..., None] * output.astype(jnp.float32), peak, total


def combine(first, second):
    highest = jnp.maximum(first[1], second[1])
    scale_one = jnp.exp(first[1] - highest)
    scale_two = jnp.exp(second[1] - highest)
    summed = first[0] * scale_one[..., None] + second[0] * scale_two[..., None]
    return summed, highest, first[2] * scale_one + second[2] * scale_two


def reference(queries, keys, values, bank, seeds, reach):
    scale = HD ** -0.5
    vectors = bank[seeds]
    transforms = jax.vmap(jax.vmap(reflect))(vectors)
    query_all = queries.reshape(SHARDS, SHARD, HEADS, HD)
    key_all = keys.reshape(SHARDS, SHARD, HEADS, HD)
    value_all = values.reshape(SHARDS, SHARD, HEADS, HD)
    places = jnp.arange(SHARD, dtype=jnp.int32)
    causal = places[:, None] >= places[None, :]

    def one_shard(shard):
        query_heads = query_all[shard]
        output, peak, total = attend_block(query_heads, key_all[shard], value_all[shard], causal, scale)
        state = (total[..., None] * output.astype(jnp.float32), peak, total)
        walked = query_heads
        for distance in range(1, WINDOW + 1):
            source = jnp.maximum(shard - distance + 1, 0).astype(jnp.int32)
            walked = jnp.einsum("thx,hxy->thy", walked.astype(jnp.float32), transforms[source],
                                precision=lax.Precision.HIGHEST).astype(jnp.bfloat16)
            earlier = jnp.maximum(shard - distance, 0).astype(jnp.int32)
            output, peak, total = attend_block(walked, key_all[earlier], value_all[earlier], None, scale)
            live = (reach >= distance) & (shard >= distance)
            state = combine(state, weigh(output, peak, total, live))
        return (state[0] / state[2][..., None]).astype(jnp.bfloat16)

    result = lax.map(one_shard, jnp.arange(SHARDS, dtype=jnp.int32))
    return result.reshape(SEQLEN, HEADS * HD)
```

```python
import functools
import math

import jax
import jax.numpy as jnp
from jax import lax
from jax.experimental import pallas as pl
from jax.experimental.pallas import tpu as pltpu
from jax.sharding import PartitionSpec as P

WINDOW = 8
GROUP = 2
LOW = -1e30
NT = (((1,), (1,)), ((), ()))
TN = (((0,), (0,)), ((), ()))
HIGH = lax.Precision.HIGHEST
F32 = jnp.float32
BF16 = jnp.bfloat16
MESH = pl.DeviceIdType.MESH


def split3(x):
    one = x.astype(BF16).astype(F32)
    rest = x - one
    two = rest.astype(BF16).astype(F32)
    return one, two, rest - two


def build_transforms(here, bank_ref, seeds_ref, u_ref, t_ref, heads, refl, width):
    rows = heads * refl

    def pick(h, carry):
        for r in range(refl):
            row = seeds_ref[here, h, r]
            u_ref[pl.ds(h * refl + r, 1), :] = bank_ref[pl.ds(row, 1), :]
        return carry

    lax.fori_loop(0, heads, pick, 0)
    v = u_ref[...]
    u = v * jnp.sqrt(2.0 / (jnp.sum(v * v, axis=1, keepdims=True) + 1e-6))
    gram = lax.dot_general(u, u, NT, precision=HIGH, preferred_element_type=F32)
    row = lax.broadcasted_iota(jnp.int32, (rows, rows), 0)
    col = lax.broadcasted_iota(jnp.int32, (rows, rows), 1)
    gram = jnp.where(row < col, gram, 0.0)
    eye = jnp.where(row == col, 1.0, 0.0).astype(F32)
    inverse = eye - jnp.where(row // 2 == col // 2, gram, 0.0)
    size = 2
    while size < refl:
        cross = jnp.where(
            (row // (2 * size) == col // (2 * size)) & (row // size != col // size), gram, 0.0
        )
        inner = jnp.dot(cross, inverse, precision=HIGH, preferred_element_type=F32)
        inverse = inverse - jnp.dot(inverse, inner, precision=HIGH, preferred_element_type=F32)
        size *= 2
    w = jnp.dot(inverse, u, precision=HIGH, preferred_element_type=F32)
    u1, u2, u3 = split3(u)
    w1, w2, w3 = split3(w)
    wide_row = lax.broadcasted_iota(jnp.int32, (width, width), 0)
    wide_col = lax.broadcasted_iota(jnp.int32, (width, width), 1)
    wide_eye = jnp.where(wide_row == wide_col, 1.0, 0.0).astype(F32)
    for h in range(heads):
        at = slice(h * refl, (h + 1) * refl)
        left = jnp.concatenate([u1[at], u1[at], u1[at], u2[at], u2[at], u3[at]], axis=0)
        right = jnp.concatenate([w1[at], w2[at], w3[at], w1[at], w2[at], w1[at]], axis=0)
        t = wide_eye - lax.dot_general(
            left.astype(BF16), right.astype(BF16), TN, preferred_element_type=F32
        )
        t1, t2, t3 = split3(t)
        t_ref[h] = jnp.concatenate([t1, t2, t3], axis=1).astype(BF16)


def rotate(q, t):
    width = q.shape[1]
    out = jnp.dot(q, t, preferred_element_type=F32)
    return (out[:, :width] + out[:, width : 2 * width] + out[:, 2 * width :]).astype(BF16)


def block(q, k, v, factor, allowed):
    s = lax.dot_general(q, k, NT, preferred_element_type=F32)
    if allowed is not None:
        s = jnp.where(allowed, s, LOW)
    m = jnp.max(s, axis=1, keepdims=True)
    p = jnp.exp2((s - m) * factor)
    total = jnp.sum(p, axis=1, keepdims=True)
    o = jnp.dot(p.astype(BF16), v, preferred_element_type=F32)
    return o, m * factor, total


def gated(state, live):
    o, m, total = state
    return jnp.where(live, o, 0.0), jnp.where(live, m, LOW), jnp.where(live, total, 0.0)


def merge(first, second):
    o1, m1, l1 = first
    o2, m2, l2 = second
    m = jnp.maximum(m1, m2)
    a1 = jnp.exp2(m1 - m)
    a2 = jnp.exp2(m2 - m)
    return o1 * a1 + o2 * a2, m, l1 * a1 + l2 * a2


def kernel(
    n, slots, q_hbm, k_hbm, v_hbm, bank_ref, seeds_ref, reach_ref, out_ref,
    q_ref, kb, vb, k0, v0, u_ref, t_ref, qr, qs, orx, osx, str_, sts, acc, ms, ls,
    load_sem, ex_send, ex_recv, kv_send, kv_recv, re_send, re_recv,
    q_send, q_recv, o_send, o_recv, s_send, s_recv,
):
    length, columns = q_ref.shape
    heads, refl = seeds_ref.shape[1:]
    width = columns // heads
    chunks = heads // GROUP
    wide = GROUP * width
    factor = width ** (-0.5) * math.log2(math.e)
    here = lax.axis_index("seq")
    half = lax.axis_index("sub")
    partner = {"sub": 1 - half}
    below = {"seq": here - 1}
    above = {"seq": here + 1}
    rows = pl.ds(pl.multiple_of(half * length, length), length)
    reached = jnp.where(here >= 1, jnp.minimum(slots, n - 1 - here), 0)

    def cols(g):
        return pl.ds(pl.multiple_of(g * wide, wide), wide)

    def head_cols(h):
        return pl.ds(pl.multiple_of(h * width, width), width)

    loads = [
        pltpu.make_async_copy(q_hbm, q_ref, load_sem.at[0]),
        pltpu.make_async_copy(k_hbm, kb.at[rows, :], load_sem.at[1]),
        pltpu.make_async_copy(v_hbm, vb.at[rows, :], load_sem.at[2]),
    ]
    for c in loads:
        c.start()

    barrier = pltpu.get_barrier_semaphore()
    pl.semaphore_signal(barrier, inc=1, device_id=partner, device_id_type=MESH)

    @pl.when(here > 0)
    def _():
        pl.semaphore_signal(barrier, inc=1, device_id=below, device_id_type=MESH)

    @pl.when(here < n - 1)
    def _():
        pl.semaphore_signal(barrier, inc=1, device_id=above, device_id_type=MESH)

    pl.semaphore_wait(
        barrier, 1 + jnp.where(here > 0, 1, 0) + jnp.where(here < n - 1, 1, 0)
    )

    def exchange(i):
        src, dst = ((k_hbm, kb), (v_hbm, vb))[i]
        return pltpu.make_async_remote_copy(
            src_ref=src, dst_ref=dst.at[rows, :], send_sem=ex_send.at[i],
            recv_sem=ex_recv.at[i], device_id=partner, device_id_type=MESH)

    def first_kv(i, g):
        src, dst = ((k_hbm, k0), (v_hbm, v0))[i]
        return pltpu.make_async_remote_copy(
            src_ref=src.at[:, cols(g)], dst_ref=dst.at[rows, cols(g)],
            send_sem=kv_send.at[i, g], recv_sem=kv_recv.at[i, g],
            device_id=above, device_id_type=MESH)

    def relay(i, g):
        buf = (k0, v0)[i]
        return pltpu.make_async_remote_copy(
            src_ref=buf.at[rows, cols(g)], dst_ref=buf.at[rows, cols(g)],
            send_sem=re_send.at[i, g], recv_sem=re_recv.at[i, g],
            device_id=partner, device_id_type=MESH)

    def send_q(slot, g):
        return pltpu.make_async_remote_copy(
            src_ref=qs.at[slot, :, cols(g)], dst_ref=qr.at[slot, :, cols(g)],
            send_sem=q_send.at[slot, g], recv_sem=q_recv.at[slot, g],
            device_id=below, device_id_type=MESH)

    def send_o(slot, g):
        return pltpu.make_async_remote_copy(
            src_ref=osx.at[slot, :, cols(g)], dst_ref=orx.at[slot, :, cols(g)],
            send_sem=o_send.at[slot, g], recv_sem=o_recv.at[slot, g],
            device_id=above, device_id_type=MESH)

    def send_s(slot, g):
        return pltpu.make_async_remote_copy(
            src_ref=sts.at[slot, g], dst_ref=str_.at[slot, g],
            send_sem=s_send.at[slot, g], recv_sem=s_recv.at[slot, g],
            device_id=above, device_id_type=MESH)

    def loop(count, body):
        def step(i, carry):
            body(i)
            return carry
        lax.fori_loop(0, count, step, 0)

    exchange(0).start()
    exchange(1).start()

    @pl.when(here == 0)
    def _():
        def go(g):
            first_kv(0, g).start()
            first_kv(1, g).start()
        loop(chunks, go)

    for c in loads:
        c.wait()

    @pl.when(here >= 1)
    def _():
        build_transforms(here, bank_ref, seeds_ref, u_ref, t_ref, heads, refl, width)

    @pl.when(here >= 2)
    def _():
        def walk(g):
            for j in range(GROUP):
                h = g * GROUP + j
                qs[0, :, head_cols(h)] = rotate(q_ref[:, head_cols(h)], t_ref[h])
            send_q(0, g).start()

            def onward(i):
                send_q(i, g).wait_recv()

                @pl.when(i + 1 < slots)
                def _():
                    for j in range(GROUP):
                        h = g * GROUP + j
                        qs[i + 1, :, head_cols(h)] = rotate(qr[i, :, head_cols(h)], t_ref[h])
                    send_q(i + 1, g).start()
            loop(reached, onward)
        loop(chunks, walk)

    exchange(0).wait_recv()
    exchange(1).wait_recv()

    place = half * length + lax.broadcasted_iota(jnp.int32, (length, 2 * length), 0)
    allowed = place >= lax.broadcasted_iota(jnp.int32, (length, 2 * length), 1)

    def own(g):
        for j in range(GROUP):
            h = g * GROUP + j
            at = head_cols(h)
            o, m, total = block(q_ref[:, at], kb[:, at], vb[:, at], factor, allowed)
            acc[:, at] = o
            ms[h] = m
            ls[h] = total
    loop(chunks, own)

    def finish(h, state):
        o, m, total = state
        out_ref[:, head_cols(h)] = (o / total).astype(BF16)

    def give(slot, g, states):
        lane = lax.broadcasted_iota(jnp.int32, (length, 128), 1)
        packed = jnp.zeros((length, 128), F32)
        for j, (o, m, total) in enumerate(states):
            osx[slot, :, head_cols(g * GROUP + j)] = (o / jnp.maximum(total, 1.0)).astype(BF16)
            packed = jnp.where(lane == 2 * j, m, packed)
            packed = jnp.where(lane == 2 * j + 1, total, packed)
        padded = sts.shape[3]
        packed = jnp.concatenate([packed, jnp.zeros((padded - length, 128), F32)], axis=0)
        sts[slot, g] = packed.T[: sts.shape[2]]
        send_o(slot, g).start()
        send_s(slot, g).start()

    def take(slot, g):
        send_o(slot, g).wait_recv()
        send_s(slot, g).wait_recv()
        stats = str_[slot, g]
        stats = jnp.concatenate(
            [stats, jnp.zeros((128 - stats.shape[0], stats.shape[1]), F32)], axis=0
        ).T[:length]
        states = []
        for j in range(GROUP):
            m = stats[:, 2 * j : 2 * j + 1]
            total = stats[:, 2 * j + 1 : 2 * j + 2]
            o = orx[slot, :, head_cols(g * GROUP + j)].astype(F32) * total
            states.append((o, m, total))
        return states

    @pl.when(here == 0)
    def _():
        def last(g):
            for j in range(GROUP):
                h = g * GROUP + j
                finish(h, (acc[:, head_cols(h)], ms[h], ls[h]))
        loop(chunks, last)

    @pl.when(here == 1)
    def _():
        def pass_on(g):
            for i in range(2):
                first_kv(i, g).wait_recv()
                relay(i, g).start()

        pass_on(0)

        def work(g):
            for i in range(2):
                relay(i, g).wait_recv()
            for j in range(GROUP):
                h = g * GROUP + j
                at = head_cols(h)
                w = rotate(q_ref[:, at], t_ref[h])
                far = gated(block(w, k0[:, at], v0[:, at], factor, None), reach_ref[h] >= 1)
                finish(h, merge((acc[:, at], ms[h], ls[h]), far))

            @pl.when(g + 1 < chunks)
            def _():
                pass_on(g + 1)

            def guest(i):
                if n > 2:
                    send_q(i, g).wait_recv()
                    states = []
                    for j in range(GROUP):
                        h = g * GROUP + j
                        at = head_cols(h)
                        w = qr[i, :, at]
                        near = gated(
                            block(w, kb[:, at], vb[:, at], factor, None), reach_ref[h] >= i + 1
                        )
                        w = rotate(w, t_ref[h])
                        far = gated(
                            block(w, k0[:, at], v0[:, at], factor, None),
                            (reach_ref[h] >= i + 2) & (i + 2 <= WINDOW),
                        )
                        states.append(merge(near, far))
                    give(i, g, states)
            loop(reached, guest)
        loop(chunks, work)

    @pl.when(here >= 2)
    def _():
        def work(g):
            def guest(i):
                states = []
                for j in range(GROUP):
                    h = g * GROUP + j
                    at = head_cols(h)
                    state = block(qr[i, :, at], kb[:, at], vb[:, at], factor, None)
                    o, m, total = gated(state, reach_ref[h] >= i + 1)
                    acc2 = (o, m, total)
                    states.append(acc2)

                if slots > 1:
                    @pl.when(i + 1 < slots)
                    def _():
                        below_states = take(i + 1, g)
                        give(i, g, [merge(a, b) for a, b in zip(states, below_states)])

                @pl.when(i + 1 >= slots)
                def _():
                    give(i, g, states)
            loop(reached, guest)
            own_below = take(0, g)
            for j in range(GROUP):
                h = g * GROUP + j
                finish(h, merge((acc[:, head_cols(h)], ms[h], ls[h]), own_below[j]))
        loop(chunks, work)

    exchange(0).wait_send()
    exchange(1).wait_send()

    @pl.when(here == 0)
    def _():
        def done(g):
            first_kv(0, g).wait_send()
            first_kv(1, g).wait_send()
        loop(chunks, done)

    @pl.when(here == 1)
    def _():
        def done(g):
            relay(0, g).wait_send()
            relay(1, g).wait_send()
        loop(chunks, done)

    def done(g):
        def back(i):
            send_o(i, g).wait_send()
            send_s(i, g).wait_send()
        loop(reached, back)

        @pl.when(here >= 2)
        def _():
            loop(jnp.minimum(reached + 1, slots), lambda i: send_q(i, g).wait_send())
    loop(chunks, done)


def shards(n, queries, keys, values, bank, seeds, reach):
    length, columns = queries.shape
    heads, refl = seeds.shape[1:]
    width = columns // heads
    chunks = heads // GROUP
    slots = max(1, min(WINDOW, n - 2))
    stat = (slots, chunks, 8, 128 * pl.cdiv(length, 128))
    anywhere = pl.BlockSpec(memory_space=pl.ANY)
    return pl.pallas_call(
        functools.partial(kernel, n, slots),
        out_shape=jax.ShapeDtypeStruct((length, columns), BF16),
        in_specs=[
            anywhere,
            anywhere,
            anywhere,
            pl.BlockSpec(memory_space=pltpu.VMEM),
            pl.BlockSpec(memory_space=pltpu.SMEM),
            pl.BlockSpec(memory_space=pltpu.SMEM),
        ],
        out_specs=pl.BlockSpec(memory_space=pltpu.VMEM),
        scratch_shapes=[
            pltpu.VMEM((length, columns), BF16),
            pltpu.VMEM((2 * length, columns), BF16),
            pltpu.VMEM((2 * length, columns), BF16),
            pltpu.VMEM((2 * length, columns), BF16),
            pltpu.VMEM((2 * length, columns), BF16),
            pltpu.VMEM((heads * refl, width), F32),
            pltpu.VMEM((heads, width, 3 * width), BF16),
            pltpu.VMEM((slots, length, columns), BF16),
            pltpu.VMEM((slots, length, columns), BF16),
            pltpu.VMEM((slots, length, columns), BF16),
            pltpu.VMEM((slots, length, columns), BF16),
            pltpu.VMEM(stat, F32),
            pltpu.VMEM(stat, F32),
            pltpu.VMEM((length, columns), F32),
            pltpu.VMEM((heads, length, 1), F32),
            pltpu.VMEM((heads, length, 1), F32),
            pltpu.SemaphoreType.DMA((3,)),
            pltpu.SemaphoreType.DMA((2,)),
            pltpu.SemaphoreType.DMA((2,)),
            pltpu.SemaphoreType.DMA((2, chunks)),
            pltpu.SemaphoreType.DMA((2, chunks)),
            pltpu.SemaphoreType.DMA((2, chunks)),
            pltpu.SemaphoreType.DMA((2, chunks)),
            pltpu.SemaphoreType.DMA((slots, chunks)),
            pltpu.SemaphoreType.DMA((slots, chunks)),
            pltpu.SemaphoreType.DMA((slots, chunks)),
            pltpu.SemaphoreType.DMA((slots, chunks)),
            pltpu.SemaphoreType.DMA((slots, chunks)),
            pltpu.SemaphoreType.DMA((slots, chunks)),
        ],
        compiler_params=pltpu.CompilerParams(
            collective_id=0, has_side_effects=True, vmem_limit_bytes=56 * 2**20
        ),
    )(queries, keys, values, bank, seeds, reach)


def solution(mesh):
    return jax.shard_map(
        functools.partial(shards, mesh.shape["seq"]),
        mesh=mesh,
        in_specs=(
            P(("parts", "seq", "sub"), "head"),
            P(("parts", "seq", "sub"), "head"),
            P(("parts", "seq", "sub"), "head"),
            P(),
            P("parts", "head", None),
            P(("parts", "head")),
        ),
        out_specs=P(("parts", "seq", "sub"), "head"),
        check_vma=False,
    )
```

```python
import functools
import math

import jax
import jax.numpy as jnp
from jax import lax
from jax.experimental import pallas as pl
from jax.experimental.pallas import tpu as pltpu
from jax.sharding import PartitionSpec as P

WINDOW = 8
GROUP = 1
STACK = 3
LOW = -1e30
NT = (((1,), (1,)), ((), ()))
TN = (((0,), (0,)), ((), ()))
HIGH = lax.Precision.HIGHEST
F32 = jnp.float32
BF16 = jnp.bfloat16
MESH = pl.DeviceIdType.MESH


def split3(x):
    one = x.astype(BF16).astype(F32)
    rest = x - one
    two = rest.astype(BF16).astype(F32)
    return one, two, rest - two


def build_transforms(bank_ref, seeds_ref, slot, u_ref, t_ref, heads, refl, width):
    rows = heads * refl

    def pick(h, carry):
        for r in range(refl):
            row = seeds_ref[slot, r, h]
            u_ref[pl.ds(h * refl + r, 1), :] = bank_ref[pl.ds(row, 1), :]
        return carry

    lax.fori_loop(0, heads, pick, 0)
    v = u_ref[...]
    u = v * jnp.sqrt(2.0 / (jnp.sum(v * v, axis=1, keepdims=True) + 1e-6))
    gram = lax.dot_general(u, u, NT, precision=HIGH, preferred_element_type=F32)
    row = lax.broadcasted_iota(jnp.int32, (rows, rows), 0)
    col = lax.broadcasted_iota(jnp.int32, (rows, rows), 1)
    gram = jnp.where(row < col, gram, 0.0)
    eye = jnp.where(row == col, 1.0, 0.0).astype(F32)
    inverse = eye - jnp.where(row // 2 == col // 2, gram, 0.0)
    size = 2
    while size < refl:
        cross = jnp.where(
            (row // (2 * size) == col // (2 * size)) & (row // size != col // size), gram, 0.0
        )
        inner = jnp.dot(cross, inverse, precision=HIGH, preferred_element_type=F32)
        inverse = inverse - jnp.dot(inverse, inner, precision=HIGH, preferred_element_type=F32)
        size *= 2
    w = jnp.dot(inverse, u, precision=HIGH, preferred_element_type=F32)
    u1, u2, u3 = split3(u)
    w1, w2, w3 = split3(w)
    wide_row = lax.broadcasted_iota(jnp.int32, (width, width), 0)
    wide_col = lax.broadcasted_iota(jnp.int32, (width, width), 1)
    wide_eye = jnp.where(wide_row == wide_col, 1.0, 0.0).astype(F32)
    for h in range(heads):
        at = slice(h * refl, (h + 1) * refl)
        left = jnp.concatenate([u1[at], u1[at], u1[at], u2[at], u2[at], u3[at]], axis=0)
        right = jnp.concatenate([w1[at], w2[at], w3[at], w1[at], w2[at], w1[at]], axis=0)
        t = wide_eye - lax.dot_general(
            left.astype(BF16), right.astype(BF16), TN, preferred_element_type=F32
        )
        t1, t2, t3 = split3(t)
        t_ref[slot, h] = jnp.concatenate([t1, t2, t3], axis=1).astype(BF16)


def rotate(q, t):
    width = q.shape[1]
    out = jnp.dot(q, t, preferred_element_type=F32)
    return (out[:, :width] + out[:, width : 2 * width] + out[:, 2 * width :]).astype(BF16)


def block(q, k, v, factor, allowed):
    s = lax.dot_general(q, k, NT, preferred_element_type=F32)
    if allowed is not None:
        first = jnp.where(allowed, s[: allowed.shape[0]], LOW)
        rest = s[allowed.shape[0] :]
        s = jnp.concatenate([first, rest], axis=0) if rest.shape[0] else first
    m = jnp.max(s, axis=1, keepdims=True)
    p = jnp.exp2((s - m) * factor)
    total = jnp.sum(p, axis=1, keepdims=True)
    o = jnp.dot(p.astype(BF16), v, preferred_element_type=F32)
    return o, m * factor, total


def gated(state, live):
    o, m, total = state
    return jnp.where(live, o, 0.0), jnp.where(live, m, LOW), jnp.where(live, total, 0.0)


def merge(first, second):
    o1, m1, l1 = first
    o2, m2, l2 = second
    m = jnp.maximum(m1, m2)
    a1 = jnp.exp2(m1 - m)
    a2 = jnp.exp2(m2 - m)
    return o1 * a1 + o2 * a2, m, l1 * a1 + l2 * a2


def kernel(
    n, slots, q_hbm, k_hbm, v_hbm, bank_ref, seeds_hbm, reach_ref, out_hbm,
    q_ref, kb, vb, k0, v0, u_ref, t_ref, qr, qs, orx, osx, str_, sts, acc, ms, ls, pk, out_ref, seeds_ref,
    load_sem, out_sem, ex_send, ex_recv, kv_send, kv_recv, re_send, re_recv,
    q_send, q_recv, o_send, o_recv, s_send, s_recv,
):
    length, columns = q_ref.shape
    refl, heads = seeds_ref.shape[1:]
    width = columns // heads
    chunks = heads // GROUP
    wide = GROUP * width
    factor = width ** (-0.5) * math.log2(math.e)
    here = lax.axis_index("seq")
    half = lax.axis_index("sub")
    partner = {"sub": 1 - half}
    below = {"seq": here - 1}
    above = {"seq": here + 1}
    rows = pl.ds(pl.multiple_of(half * length, length), length)
    reached = jnp.where(here >= 1, jnp.minimum(slots, n - 1 - here), 0)

    def cols(g):
        return pl.ds(pl.multiple_of(g * wide, wide), wide)

    def head_cols(h):
        return pl.ds(pl.multiple_of(h * width, width), width)

    loads = [
        pltpu.make_async_copy(q_hbm, q_ref, load_sem.at[0]),
        pltpu.make_async_copy(k_hbm, kb.at[rows, :], load_sem.at[1]),
        pltpu.make_async_copy(v_hbm, vb.at[rows, :], load_sem.at[2]),
        pltpu.make_async_copy(
            seeds_hbm.at[jnp.minimum(here + 1, n - 1)], seeds_ref.at[0], load_sem.at[3]),
        pltpu.make_async_copy(seeds_hbm.at[here], seeds_ref.at[1], load_sem.at[4]),
    ]
    for c in loads:
        c.start()

    barrier = pltpu.get_barrier_semaphore()
    pl.semaphore_signal(barrier, inc=1, device_id=partner, device_id_type=MESH)

    @pl.when(here > 0)
    def _():
        pl.semaphore_signal(barrier, inc=1, device_id=below, device_id_type=MESH)

    @pl.when(here < n - 1)
    def _():
        pl.semaphore_signal(barrier, inc=1, device_id=above, device_id_type=MESH)

    pl.semaphore_wait(
        barrier, 1 + jnp.where(here > 0, 1, 0) + jnp.where(here < n - 1, 1, 0)
    )

    def exchange(i):
        src, dst = ((k_hbm, kb), (v_hbm, vb))[i]
        return pltpu.make_async_remote_copy(
            src_ref=src, dst_ref=dst.at[rows, :], send_sem=ex_send.at[i],
            recv_sem=ex_recv.at[i], device_id=partner, device_id_type=MESH)

    def first_kv(i, g):
        src, dst = ((k_hbm, k0), (v_hbm, v0))[i]
        return pltpu.make_async_remote_copy(
            src_ref=src.at[:, cols(g)], dst_ref=dst.at[rows, cols(g)],
            send_sem=kv_send.at[i, g], recv_sem=kv_recv.at[i, g],
            device_id=above, device_id_type=MESH)

    def relay(i, g):
        buf = (k0, v0)[i]
        return pltpu.make_async_remote_copy(
            src_ref=buf.at[rows, cols(g)], dst_ref=buf.at[rows, cols(g)],
            send_sem=re_send.at[i, g], recv_sem=re_recv.at[i, g],
            device_id=partner, device_id_type=MESH)

    def send_q(slot, g):
        return pltpu.make_async_remote_copy(
            src_ref=qs.at[jnp.maximum(slot - 1, 0), :, cols(g)], dst_ref=qr.at[slot, :, cols(g)],
            send_sem=q_send.at[slot, g], recv_sem=q_recv.at[slot, g],
            device_id=below, device_id_type=MESH)

    def send_own(g):
        return pltpu.make_async_remote_copy(
            src_ref=q_hbm.at[:, cols(g)], dst_ref=qr.at[0, :, cols(g)],
            send_sem=q_send.at[0, g], recv_sem=q_recv.at[0, g],
            device_id=below, device_id_type=MESH)

    def send_o(slot, g):
        return pltpu.make_async_remote_copy(
            src_ref=osx.at[slot, :, cols(g)], dst_ref=orx.at[slot, :, cols(g)],
            send_sem=o_send.at[slot, g], recv_sem=o_recv.at[slot, g],
            device_id=above, device_id_type=MESH)

    def send_s(slot, g):
        return pltpu.make_async_remote_copy(
            src_ref=sts.at[slot, g], dst_ref=str_.at[slot, g],
            send_sem=s_send.at[slot, g], recv_sem=s_recv.at[slot, g],
            device_id=above, device_id_type=MESH)

    def loop(count, body):
        def step(i, carry):
            body(i)
            return carry
        lax.fori_loop(0, count, step, 0)

    @pl.when(here == 0)
    def _():
        def go(g):
            first_kv(0, g).start()
            first_kv(1, g).start()
        loop(chunks, go)

    @pl.when(here == n - 1)
    def _():
        if n > 2:
            loop(chunks, lambda g: send_own(g).start())

    @pl.when((here >= 2) & (here < n - 1))
    def _():
        send_own(0).start()
        send_own(1).start()

    exchange(0).start()
    exchange(1).start()
    for c in loads:
        c.wait()

    @pl.when((here >= 1) & (here < n - 1))
    def _():
        build_transforms(bank_ref, seeds_ref, 0, u_ref, t_ref, heads, refl, width)

    @pl.when(here == 1)
    def _():
        build_transforms(bank_ref, seeds_ref, 1, u_ref, t_ref, heads, refl, width)

    place = half * length + lax.broadcasted_iota(jnp.int32, (length, 2 * length), 0)
    allowed = place >= lax.broadcasted_iota(jnp.int32, (length, 2 * length), 1)

    def own(g):
        for j in range(GROUP):
            h = g * GROUP + j
            at = head_cols(h)
            o, m, total = block(q_ref[:, at], kb[:, at], vb[:, at], factor, allowed)
            acc[:, at] = o
            ms[h] = m
            ls[h] = total

    def write(g):
        return pltpu.make_async_copy(
            out_ref.at[:, cols(g)], out_hbm.at[:, cols(g)], out_sem.at[g])

    def finish(h, state):
        o, m, total = state
        out_ref[:, head_cols(h)] = (o / total).astype(BF16)

    def hold(slot, g, states):
        lane = lax.broadcasted_iota(jnp.int32, (length, 128), 1)
        packed = jnp.zeros((length, 128), F32)
        for j, (o, m, total) in enumerate(states):
            osx[slot, :, head_cols(g * GROUP + j)] = (o / jnp.maximum(total, 1.0)).astype(BF16)
            packed = jnp.where(lane == 2 * j, m, packed)
            packed = jnp.where(lane == 2 * j + 1, total, packed)
        return packed

    def give(slot, g, packed):
        padded = sts.shape[3]
        packed = jnp.concatenate([packed, jnp.zeros((padded - length, 128), F32)], axis=0)
        sts[slot, g] = packed.T[: sts.shape[2]]
        send_o(slot, g).start()
        send_s(slot, g).start()

    def unpack(ref, slot, g, stats):
        states = []
        for j in range(GROUP):
            m = stats[:, 2 * j : 2 * j + 1]
            total = stats[:, 2 * j + 1 : 2 * j + 2]
            o = ref[slot, :, head_cols(g * GROUP + j)].astype(F32) * total
            states.append((o, m, total))
        return states

    def take(slot, g):
        send_o(slot, g).wait_recv()
        send_s(slot, g).wait_recv()
        stats = str_[slot, g]
        stats = jnp.concatenate(
            [stats, jnp.zeros((128 - stats.shape[0], stats.shape[1]), F32)], axis=0
        ).T[:length]
        return unpack(orx, slot, g, stats)

    @pl.when(here == 0)
    def _():
        exchange(0).wait_recv()
        exchange(1).wait_recv()

        def last(g):
            own(g)
            for j in range(GROUP):
                h = g * GROUP + j
                finish(h, (acc[:, head_cols(h)], ms[h], ls[h]))
            write(g).start()
        loop(chunks, last)

    @pl.when(here == 1)
    def _():
        exchange(0).wait_recv()
        exchange(1).wait_recv()
        guests = list(range(slots)) if n > 2 else []
        batches = [([-1] + guests)[i : i + STACK] for i in range(0, 1 + len(guests), STACK)]

        def work(g):
            for i in range(2):
                first_kv(i, g).wait_recv()
                relay(i, g).start()
            for i in guests:
                send_q(i, g).wait_recv()
            near = []
            for j in range(GROUP):
                h = g * GROUP + j
                at = head_cols(h)
                for batch in batches:
                    w = jnp.concatenate([qr[i, :, at] for i in batch if i >= 0], axis=0) if batch != [-1] else None
                    if w is not None:
                        w = rotate(w, t_ref[0, h])
                    if batch[0] < 0:
                        w = q_ref[:, at] if w is None else jnp.concatenate([q_ref[:, at], w], axis=0)
                    state = block(
                        w, kb[:, at], vb[:, at], factor, allowed if batch[0] < 0 else None
                    )
                    near.append((state, rotate(w, t_ref[1, h])))
            for i in range(2):
                relay(i, g).wait_recv()
            ready = {i: [] for i in guests}
            for j in range(GROUP):
                h = g * GROUP + j
                at = head_cols(h)
                for b, batch in enumerate(batches):
                    first, w = near[j * len(batches) + b]
                    second = block(w, k0[:, at], v0[:, at], factor, None)
                    for e, i in enumerate(batch):
                        part = slice(e * length, (e + 1) * length)
                        a = tuple(x[part] for x in first)
                        z = tuple(x[part] for x in second)
                        z = gated(z, (reach_ref[h] >= i + 2) & (i + 2 <= WINDOW))
                        if i < 0:
                            finish(h, merge(a, z))
                        else:
                            ready[i].append(merge(gated(a, reach_ref[h] >= i + 1), z))
            for i in reversed(guests):
                give(i, g, hold(i, g, ready[i]))
            write(g).start()
        loop(chunks, work)

    @pl.when(here >= 2)
    def _():
        def walk(g):
            @pl.when((here < n - 1) & (g + 2 < chunks))
            def _():
                send_own(g + 2).start()

            @pl.when(g == 0)
            def _():
                exchange(0).wait_recv()
                exchange(1).wait_recv()

            def onward(i):
                send_q(i, g).wait_recv()
                for j in range(GROUP):
                    h = g * GROUP + j
                    qs[i, :, head_cols(h)] = rotate(qr[i, :, head_cols(h)], t_ref[0, h])

                @pl.when(i + 1 < slots)
                def _():
                    send_q(i + 1, g).start()

                states = []
                for j in range(GROUP):
                    h = g * GROUP + j
                    at = head_cols(h)
                    state = block(qs[i, :, at], kb[:, at], vb[:, at], factor, None)
                    states.append(gated(state, reach_ref[h] >= i + 1))
                packed = hold(i, g, states)
                pk[i, g] = packed

                @pl.when(i + 1 >= slots)
                def _():
                    give(i, g, packed)
            loop(reached, onward)
            own(g)
        loop(chunks, walk)

        def work(g):
            def guest(k):
                i = reached - 1 - k

                @pl.when(i + 1 < slots)
                def _():
                    ahead = take(i + 1, g)
                    mine = unpack(osx, i, g, pk[i, g])
                    give(i, g, hold(i, g, [merge(a, b) for a, b in zip(mine, ahead)]))
            loop(reached, guest)
            ahead = take(0, g)
            for j in range(GROUP):
                h = g * GROUP + j
                finish(h, merge((acc[:, head_cols(h)], ms[h], ls[h]), ahead[j]))
            write(g).start()
        loop(chunks, work)

    loop(chunks, lambda g: write(g).wait())
    exchange(0).wait_send()
    exchange(1).wait_send()

    @pl.when(here == 0)
    def _():
        def done(g):
            first_kv(0, g).wait_send()
            first_kv(1, g).wait_send()
        loop(chunks, done)

    @pl.when(here == 1)
    def _():
        def done(g):
            relay(0, g).wait_send()
            relay(1, g).wait_send()
        loop(chunks, done)

    def done(g):
        def back(i):
            send_o(i, g).wait_send()
            send_s(i, g).wait_send()
        loop(reached, back)

        @pl.when(here >= 2)
        def _():
            loop(jnp.minimum(reached + 1, slots), lambda i: send_q(i, g).wait_send())
    loop(chunks, done)


def shards(n, queries, keys, values, bank, seeds, reach):
    length, columns = queries.shape
    heads, refl = seeds.shape[1:]
    seeds = jnp.swapaxes(seeds, 1, 2)
    width = columns // heads
    chunks = heads // GROUP
    slots = max(1, min(WINDOW, n - 2))
    stat = (slots, chunks, 2 * GROUP, 128 * pl.cdiv(length, 128))
    anywhere = pl.BlockSpec(memory_space=pl.ANY)
    return pl.pallas_call(
        functools.partial(kernel, n, slots),
        out_shape=jax.ShapeDtypeStruct((length, columns), BF16),
        in_specs=[
            anywhere,
            anywhere,
            anywhere,
            pl.BlockSpec(memory_space=pltpu.VMEM),
            anywhere,
            pl.BlockSpec(memory_space=pltpu.SMEM),
        ],
        out_specs=anywhere,
        scratch_shapes=[
            pltpu.VMEM((length, columns), BF16),
            pltpu.VMEM((2 * length, columns), BF16),
            pltpu.VMEM((2 * length, columns), BF16),
            pltpu.VMEM((2 * length, columns), BF16),
            pltpu.VMEM((2 * length, columns), BF16),
            pltpu.VMEM((heads * refl, width), F32),
            pltpu.VMEM((2, heads, width, 3 * width), BF16),
            pltpu.VMEM((slots, length, columns), BF16),
            pltpu.VMEM((slots, length, columns), BF16),
            pltpu.VMEM((slots, length, columns), BF16),
            pltpu.VMEM((slots, length, columns), BF16),
            pltpu.VMEM(stat, F32),
            pltpu.VMEM(stat, F32),
            pltpu.VMEM((length, columns), F32),
            pltpu.VMEM((heads, length, 1), F32),
            pltpu.VMEM((heads, length, 1), F32),
            pltpu.VMEM((slots, chunks, length, 128), F32),
            pltpu.VMEM((length, columns), BF16),
            pltpu.SMEM((2, refl, heads), jnp.int32),
            pltpu.SemaphoreType.DMA((5,)),
            pltpu.SemaphoreType.DMA((chunks,)),
            pltpu.SemaphoreType.DMA((2,)),
            pltpu.SemaphoreType.DMA((2,)),
            pltpu.SemaphoreType.DMA((2, chunks)),
            pltpu.SemaphoreType.DMA((2, chunks)),
            pltpu.SemaphoreType.DMA((2, chunks)),
            pltpu.SemaphoreType.DMA((2, chunks)),
            pltpu.SemaphoreType.DMA((slots, chunks)),
            pltpu.SemaphoreType.DMA((slots, chunks)),
            pltpu.SemaphoreType.DMA((slots, chunks)),
            pltpu.SemaphoreType.DMA((slots, chunks)),
            pltpu.SemaphoreType.DMA((slots, chunks)),
            pltpu.SemaphoreType.DMA((slots, chunks)),
        ],
        compiler_params=pltpu.CompilerParams(
            collective_id=0, has_side_effects=True, vmem_limit_bytes=56 * 2**20
        ),
    )(queries, keys, values, bank, seeds, reach)


def solution(mesh):
    return jax.shard_map(
        functools.partial(shards, mesh.shape["seq"]),
        mesh=mesh,
        in_specs=(
            P(("parts", "seq", "sub"), "head"),
            P(("parts", "seq", "sub"), "head"),
            P(("parts", "seq", "sub"), "head"),
            P(),
            P("parts", "head", None),
            P(("parts", "head")),
        ),
        out_specs=P(("parts", "seq", "sub"), "head"),
        check_vma=False,
    )
```
